32 devices in a mesh: pool: 16 (over z, y, core), tensor: 2 (over x).
Axes of the slice: x: 2, y: 2, z: 4, core: 2. Of those that a mesh axis runs over, the one named last changes fastest.
Arguments:
- queries: bfloat16 [2048, 4096], P(('pool', 'tensor')), may hold values from -6 to 6
- incoming_keys: bfloat16 [2048, 2048], P(('pool', 'tensor')), may hold values from -6 to 6
- incoming_values: bfloat16 [2048, 2048], P(('pool', 'tensor')), may hold values from -6 to 6
- cached_key_pages: bfloat16 [256, 128, 2048], P('pool', None, 'tensor'), may hold values from -6 to 6
- cached_value_pages: bfloat16 [256, 128, 2048], P('pool', None, 'tensor'), may hold values from -6 to 6
- page_table: int32 [16, 64], replicated, may hold values from -1 to 255, as said below
- lengths: int32 [16], replicated, may hold values from 1 to 8192, as said below
Outputs:
- attended: bfloat16 [2048, 4096], P(('pool', 'tensor'))
The draws below stay inside these ranges and needn't reach their ends.
Inputs may be any that keep to these rules, and one draw needn't show every extreme that they name: Request r has ceil(lengths[r] / 128) pages; for j below that, page_table[r, j] is the slot of its page j, a slot g of pool device g // 16, which is one of r, r + 1, ..., r + 3 counted modulo 16. No slot holds two pages. All other entries are -1. `lengths`: some request has exactly 8192 cached tokens.
All inputs are finite; a program needn't handle non-finite values.
Results may differ from the reference program's by a relative error of at most 0.008.
Values may be sent and summed in bfloat16 or wider, within the bound.
A program may use at most 64 MiB of HBM per device.

```python
import jax
import jax.numpy as jnp
from jax import lax

QUERY_HEADS = 16
KEY_VALUE_HEADS = 8
HEAD_SIZE = 256
REQUEST_TOKENS = 128
PAGE_TOKENS = 128
SPAN = 4
POOL_PAGE_SLOTS = 16
REQUEST_COUNT = 16
NEW_TOKEN_COUNT = 2048
TOTAL_SLOTS = 256
MAXP = 64
N_POOL = 16


def draw_layout(key):
    folded = jax.random.fold_in(key, 7)
    star_key, which_key, fill_key, alive_key, order_key, length_key = jax.random.split(folded, 6)
    slot_total = REQUEST_COUNT * POOL_PAGE_SLOTS
    holder = jnp.arange(slot_total, dtype=jnp.int32) // POOL_PAGE_SLOTS
    position = jnp.arange(slot_total, dtype=jnp.int32) % POOL_PAGE_SLOTS
    longest = jax.random.randint(star_key, (), 0, REQUEST_COUNT).astype(jnp.int32)
    distance = jax.random.randint(which_key, (slot_total,), 0, SPAN).astype(jnp.int32)
    fill_level = jax.random.randint(fill_key, (REQUEST_COUNT,), 3, 11)
    alive = jax.random.randint(alive_key, (slot_total,), 0, 10) < fill_level[holder]
    alive = alive | (position == POOL_PAGE_SLOTS - 1) | (position == 0)
    distance = jnp.where(position == 0, 0, distance)
    offset = (holder - longest) % REQUEST_COUNT
    in_block = offset < SPAN
    next_holder = offset == SPAN
    special = next_holder & (position >= 1) & (position < SPAN)
    distance = jnp.where(special, SPAN - position, distance)
    alive = alive | special
    distance = jnp.where(in_block, offset, distance)
    alive = alive | in_block
    slot_owner = jnp.where(alive, (holder - distance) % REQUEST_COUNT, REQUEST_COUNT).astype(jnp.int32)
    priority = jax.random.permutation(order_key, slot_total).astype(jnp.int32)
    same_owner = slot_owner[:, None] == slot_owner[None, :]
    before = priority[None, :] < priority[:, None]
    page_rank = jnp.sum(same_owner & before, axis=1).astype(jnp.int32)
    table_out = jnp.full((REQUEST_COUNT + 1, MAXP), -1, jnp.int32)
    table_out = table_out.at[slot_owner, page_rank].set(jnp.arange(slot_total, dtype=jnp.int32), mode='drop')[:REQUEST_COUNT]
    page_count = jnp.sum(table_out >= 0, axis=1).astype(jnp.int32)
    last_fill = jax.random.randint(length_key, (REQUEST_COUNT,), 1, PAGE_TOKENS + 1).astype(jnp.int32)
    length_out = (page_count - 1) * PAGE_TOKENS + last_fill
    length_out = jnp.where(jnp.arange(REQUEST_COUNT, dtype=jnp.int32) == longest, MAXP * PAGE_TOKENS, length_out)
    return (table_out, length_out.astype(jnp.int32))


def draw_page_table(key, part):
    return draw_layout(key)[0]


def draw_lengths(key, part):
    return draw_layout(key)[1]


def block_scale(key, extent, pieces, least, largest):
    factor_of = 1.0
    for dim, blocks in pieces:
        steps = jax.random.uniform(jax.random.fold_in(jax.random.fold_in(key, 6), dim), (blocks,), jnp.float32, least / len(pieces), largest / len(pieces))
        factor_of = factor_of * jnp.repeat(jnp.exp(steps), extent[dim] // blocks).reshape((-1,) + (1,) * (len(extent) - 1 - dim))
    return factor_of


def noise(stream_key, extent, width, limit, pieces=(), held_as=jnp.bfloat16):
    entries = jax.random.normal(stream_key, extent, jnp.float32) * width
    if len(pieces) > 0:
        entries = block_scale(stream_key, extent, pieces, -0.22, 0.18) * entries
    return jnp.clip(entries, min=-limit, max=limit).astype(held_as)


def setup_inputs(seed: int = 0) -> dict:
    arg_keys = jax.random.split(jax.random.key(seed), 8)
    queries = noise(arg_keys[0], (NEW_TOKEN_COUNT, QUERY_HEADS * HEAD_SIZE), 1.0, 6.0, ((0, 32),))
    incoming_keys = noise(arg_keys[1], (NEW_TOKEN_COUNT, KEY_VALUE_HEADS * HEAD_SIZE), 1.0, 6.0, ((0, 32),))
    incoming_values = noise(arg_keys[2], (NEW_TOKEN_COUNT, KEY_VALUE_HEADS * HEAD_SIZE), 1.0, 6.0, ((0, 32),))
    cached_key_pages = noise(arg_keys[3], (TOTAL_SLOTS, PAGE_TOKENS, KEY_VALUE_HEADS * HEAD_SIZE), 1.0, 6.0, ((0, 16), (2, 2)))
    cached_value_pages = noise(arg_keys[4], (TOTAL_SLOTS, PAGE_TOKENS, KEY_VALUE_HEADS * HEAD_SIZE), 1.0, 6.0, ((0, 16), (2, 2)))
    page_table = draw_page_table(jax.random.fold_in(arg_keys[7], 71), 0)
    lengths = draw_lengths(jax.random.fold_in(arg_keys[7], 71), 0)
    return dict(queries=queries, incoming_keys=incoming_keys, incoming_values=incoming_values, cached_key_pages=cached_key_pages, cached_value_pages=cached_value_pages, page_table=page_table, lengths=lengths)


SOFTCAP = 50.0


def capped(scores, visible):
    capped_scores = SOFTCAP * jnp.tanh(scores / SOFTCAP)
    return jnp.where(visible, jnp.exp(capped_scores), 0.0).astype(jnp.bfloat16)


def reference(queries, incoming_keys, incoming_values, cached_key_pages, cached_value_pages, page_table, lengths):
    query_group_width = QUERY_HEADS // KEY_VALUE_HEADS
    score_scale = HEAD_SIZE ** -0.5
    query_layout_grid = queries.reshape(REQUEST_COUNT, REQUEST_TOKENS, KEY_VALUE_HEADS, query_group_width, HEAD_SIZE).astype(jnp.float32)
    fresh_key_rows = incoming_keys.reshape(REQUEST_COUNT, REQUEST_TOKENS, KEY_VALUE_HEADS, HEAD_SIZE).astype(jnp.float32)
    fresh_value_rows = incoming_values.reshape(REQUEST_COUNT, REQUEST_TOKENS, KEY_VALUE_HEADS, HEAD_SIZE).astype(jnp.float32)
    causal = jnp.arange(REQUEST_TOKENS)[None, :] <= jnp.arange(REQUEST_TOKENS)[:, None]
    own_scores = jnp.einsum('rqgah,rkgh->rgaqk', query_layout_grid, fresh_key_rows) * score_scale
    own_weights = capped(own_scores, causal).astype(jnp.float32)
    own_numer = jnp.einsum('rgaqk,rkgh->rqgah', own_weights, fresh_value_rows)
    own_total = jnp.sum(own_weights, axis=-1)

    flat_table = page_table.reshape(-1)
    request_ids = jnp.repeat(jnp.arange(REQUEST_COUNT, dtype=jnp.int32), MAXP)
    page_ids = jnp.tile(jnp.arange(MAXP, dtype=jnp.int32), REQUEST_COUNT)
    target = jnp.where(flat_table >= 0, flat_table, TOTAL_SLOTS).astype(jnp.int32)
    slot_owner = jnp.full((TOTAL_SLOTS,), REQUEST_COUNT, jnp.int32).at[target].set(request_ids, mode='drop')
    slot_page = jnp.zeros((TOTAL_SLOTS,), jnp.int32).at[target].set(page_ids, mode='drop')
    slot_limit = jnp.where(slot_owner < REQUEST_COUNT, jnp.take(lengths, jnp.minimum(slot_owner, REQUEST_COUNT - 1)), 0).astype(jnp.int32)

    def one_block(running, input_arrays):
        key_page_block, value_page_block, owner_block, page_block, limit_block = input_arrays
        query_pick = jnp.take(query_layout_grid, jnp.minimum(owner_block, REQUEST_COUNT - 1), axis=0)
        key_layout_grid = key_page_block.reshape(POOL_PAGE_SLOTS, PAGE_TOKENS, KEY_VALUE_HEADS, HEAD_SIZE).astype(jnp.float32)
        value_layout_grid = value_page_block.reshape(POOL_PAGE_SLOTS, PAGE_TOKENS, KEY_VALUE_HEADS, HEAD_SIZE).astype(jnp.float32)
        scores = jnp.einsum('bqgah,bkgh->bgaqk', query_pick, key_layout_grid) * score_scale
        position = page_block[:, None] * PAGE_TOKENS + jnp.arange(PAGE_TOKENS, dtype=jnp.int32)[None, :]
        visible = position < limit_block[:, None]
        weights = capped(scores, visible[:, None, None, None, :]).astype(jnp.float32)
        numer = jnp.einsum('bgaqk,bkgh->bqgah', weights, value_layout_grid)
        totals = jnp.sum(weights, axis=-1)
        numer_acc, total_acc = running
        return (numer_acc.at[owner_block].add(numer), total_acc.at[owner_block].add(totals)), None

    start_offset = (jnp.zeros((REQUEST_COUNT + 1, REQUEST_TOKENS, KEY_VALUE_HEADS, query_group_width, HEAD_SIZE), jnp.float32),
             jnp.zeros((REQUEST_COUNT + 1, KEY_VALUE_HEADS, query_group_width, REQUEST_TOKENS), jnp.float32))
    input_arrays = (cached_key_pages.reshape(N_POOL, POOL_PAGE_SLOTS, PAGE_TOKENS, KEY_VALUE_HEADS * HEAD_SIZE),
              cached_value_pages.reshape(N_POOL, POOL_PAGE_SLOTS, PAGE_TOKENS, KEY_VALUE_HEADS * HEAD_SIZE),
              slot_owner.reshape(N_POOL, POOL_PAGE_SLOTS),
              slot_page.reshape(N_POOL, POOL_PAGE_SLOTS),
              slot_limit.reshape(N_POOL, POOL_PAGE_SLOTS))
    (numer_acc, total_acc), _ = lax.scan(one_block, start_offset, input_arrays)
    numerator = numer_acc[:REQUEST_COUNT] + own_numer
    totals = jnp.transpose(total_acc[:REQUEST_COUNT] + own_total, (0, 3, 1, 2))
    attended = numerator / totals[..., None]
    return attended.reshape(NEW_TOKEN_COUNT, QUERY_HEADS * HEAD_SIZE).astype(jnp.bfloat16)
```

```python
import functools
import math

import jax
import jax.numpy as jnp
from jax import lax
from jax.experimental import pallas as pl
from jax.experimental.pallas import tpu as pltpu
from jax.sharding import PartitionSpec as P

QUERY_HEADS = 16
KEY_VALUE_HEADS = 8
HEAD_SIZE = 256
SPAN = 4
SOFTCAP = 50.0

GROUP = QUERY_HEADS // KEY_VALUE_HEADS
WIDE = GROUP * HEAD_SIZE
INNER = HEAD_SIZE ** (-0.5) / SOFTCAP
OUTER = SOFTCAP * math.log2(math.e)
MESH = pl.DeviceIdType.MESH


def rows_by_head(block):
    return jnp.concatenate(
        [block[:, g * HEAD_SIZE : (g + 1) * HEAD_SIZE] for g in range(GROUP)], axis=0
    )


def tokens_by_head(block):
    n = block.shape[0] // GROUP
    return jnp.concatenate([block[g * n : (g + 1) * n] for g in range(GROUP)], axis=1)


def weigh(query, key):
    dots = lax.dot_general(query, key, (((1,), (1,)), ((), ())), preferred_element_type=jnp.float32)
    return jnp.exp2(OUTER * jnp.tanh(dots * INNER))


def kernel(
    n_pool,
    n_tensor,
    heads,
    dist,
    mask_rows,
    mask_each,
    q_in,
    k_in,
    v_in,
    k_pages,
    v_pages,
    out,
    *scratch,
):
    qbufs = scratch[:heads]
    (
        k_own,
        v_own,
        k_mem,
        v_mem,
        weights,
        own_numer,
        own_total,
        numer_out,
        total_out,
        numer_in,
        total_in,
        done,
        page_sem,
        local_sem,
        qx_send,
        qx_recv,
        kx_send,
        kx_recv,
        qf_send,
        qf_recv,
        nr_send,
        nr_recv,
        tr_send,
        tr_recv,
        ox_send,
        ox_recv,
    ) = scratch[heads:]
    p = lax.axis_index("pool")
    t = lax.axis_index("tensor")
    rows = q_in.shape[0]
    tokens = rows * n_tensor
    slots = k_pages.shape[0]
    page = k_pages.shape[1]
    span_cols = heads * HEAD_SIZE

    def pool_at(d):
        return (lax.rem(p + d + n_pool, n_pool), t)

    def tensor_at(i):
        return lax.rem(t + i, n_tensor)

    page_copies = []
    for h in range(heads):
        cols = slice(h * HEAD_SIZE, (h + 1) * HEAD_SIZE)
        page_copies.append(
            [
                pltpu.make_async_copy(k_pages.at[:, :, cols], k_mem.at[h], page_sem.at[h, 0]),
                pltpu.make_async_copy(v_pages.at[:, :, cols], v_mem.at[h], page_sem.at[h, 1]),
            ]
        )

    my_rows = pl.ds(pl.multiple_of(t * rows, rows), rows)

    def q_cols(owner, h):
        return pl.ds(pl.multiple_of((owner * heads + h) * WIDE, WIDE), WIDE)

    local = []
    for h in range(heads):
        local.append(
            pltpu.make_async_copy(
                q_in.at[:, q_cols(t, h)], qbufs[h].at[0, my_rows, :], local_sem.at[h]
            )
        )
    own_cols = pl.ds(pl.multiple_of(t * span_cols, span_cols), span_cols)
    local_kv = [
        pltpu.make_async_copy(k_in.at[:, own_cols], k_own.at[my_rows, :], local_sem.at[heads]),
        pltpu.make_async_copy(v_in.at[:, own_cols], v_own.at[my_rows, :], local_sem.at[heads + 1]),
    ]
    for c in local:
        c.start()
    for c in page_copies[0]:
        c.start()

    barrier = pltpu.get_barrier_semaphore()
    for i in range(1, n_tensor):
        pl.semaphore_signal(barrier, inc=1, device_id=(p, tensor_at(i)), device_id_type=MESH)
    for d in range(1, SPAN):
        pl.semaphore_signal(barrier, inc=1, device_id=pool_at(d), device_id_type=MESH)
        pl.semaphore_signal(barrier, inc=1, device_id=pool_at(-d), device_id_type=MESH)
    pl.semaphore_wait(barrier, n_tensor - 1 + 2 * (SPAN - 1))

    def remote(src, dst, send, recv, device):
        return pltpu.make_async_remote_copy(
            src_ref=src,
            dst_ref=dst,
            send_sem=send,
            recv_sem=recv,
            device_id=device,
            device_id_type=MESH,
        )

    exchange = []
    for h in range(heads):
        exchange.append(
            [
                remote(
                    q_in.at[:, q_cols(tensor_at(i), h)],
                    qbufs[h].at[0, my_rows, :],
                    qx_send.at[h, i],
                    qx_recv.at[h, i],
                    (p, tensor_at(i)),
                )
                for i in range(1, n_tensor)
            ]
        )
        for c in exchange[h]:
            c.start()
    exchange_kv = []
    for i in range(1, n_tensor):
        their_cols = pl.ds(pl.multiple_of(tensor_at(i) * span_cols, span_cols), span_cols)
        for j, (src, dst) in enumerate(((k_in, k_own), (v_in, v_own))):
            exchange_kv.append(
                remote(
                    src.at[:, their_cols],
                    dst.at[my_rows, :],
                    kx_send.at[j, i],
                    kx_recv.at[j, i],
                    (p, tensor_at(i)),
                )
            )
    for c in local_kv:
        c.start()
    for c in exchange_kv:
        c.start()
    for pair in page_copies[1:]:
        for c in pair:
            c.start()

    forward = []
    for h in range(heads):
        local[h].wait()
        for c in exchange[h]:
            c.wait_recv()
        forward.append(
            [
                remote(
                    qbufs[h].at[0],
                    qbufs[h].at[d],
                    qf_send.at[h, d],
                    qf_recv.at[h, d],
                    pool_at(d),
                )
                for d in range(1, SPAN)
            ]
        )
        for c in forward[h]:
            c.start()

    back = []
    for h in range(heads):
        for c in page_copies[h]:
            c.wait()
        for c in forward[h]:
            c.wait_recv()

        qbuf = qbufs[h]

        @pl.loop(0, slots // 4)
        def _(j):
            for u in range(4):
                s = j * 4 + u
                query = rows_by_head(qbuf[dist[s]])
                cols = pl.ds(pl.multiple_of(s * page, page), page)
                weights[:, cols] = weigh(query, k_mem[h, s]).astype(jnp.bfloat16)

        values = v_mem[h].reshape(slots * page, HEAD_SIZE)
        totals = lax.dot_general(
            mask_rows[...],
            weights[...],
            (((1,), (1,)), ((), ())),
            preferred_element_type=jnp.float32,
        )
        own_total[h] = totals
        total_out[h] = totals
        back.append([])
        for d in list(range(1, SPAN)) + [0]:
            all_weights = weights[...]
            kept = all_weights.reshape(-1, 16, slots * page) * mask_each[d][None]
            numer = jnp.dot(
                kept.reshape(all_weights.shape), values, preferred_element_type=jnp.float32
            )
            if d == 0:
                own_numer[h] = numer
            else:
                numer_out[h, d - 1] = tokens_by_head(numer.astype(jnp.bfloat16))
                pair = [
                    remote(
                        numer_out.at[h, d - 1],
                        numer_in.at[h, d - 1],
                        nr_send.at[h, d],
                        nr_recv.at[h, d],
                        pool_at(-d),
                    ),
                    remote(
                        total_out.at[h],
                        total_in.at[h, d - 1],
                        tr_send.at[h, d],
                        tr_recv.at[h, d],
                        pool_at(-d),
                    ),
                ]
                for c in pair:
                    c.start()
                back[h] += pair

    for c in local_kv:
        c.wait()
    for c in exchange_kv:
        c.wait_recv()
    n_rows = GROUP * tokens
    query_token = lax.broadcasted_iota(jnp.int32, (n_rows, tokens), 0) % tokens
    causal = lax.broadcasted_iota(jnp.int32, (n_rows, tokens), 1) <= query_token
    ones = jnp.ones((16, tokens), jnp.bfloat16)
    for h in range(heads):
        cols = slice(h * HEAD_SIZE, (h + 1) * HEAD_SIZE)
        fresh = jnp.where(causal, weigh(rows_by_head(qbufs[h][0]), k_own[:, cols]), 0.0)
        fresh = fresh.astype(jnp.bfloat16)
        own_numer[h] += jnp.dot(fresh, v_own[:, cols], preferred_element_type=jnp.float32)
        own_total[h] += lax.dot_general(
            ones, fresh, (((1,), (1,)), ((), ())), preferred_element_type=jnp.float32
        )

    finished = []
    for h in range(heads):
        for c in back[h]:
            c.wait_recv()
        total = own_total[h, 0:1, :]
        numer = own_numer[h]
        for d in range(1, SPAN):
            total = total + total_in[h, d - 1, d : d + 1, :]
            numer = numer + rows_by_head(numer_in[h, d - 1].astype(jnp.float32))
        per_row = jnp.broadcast_to(total, (128, n_rows)).T
        per_row = jnp.concatenate([per_row] * (HEAD_SIZE // 128), axis=1)
        done[h] = tokens_by_head((numer / per_row).astype(jnp.bfloat16))
        mine = pltpu.make_async_copy(
            done.at[h, my_rows, :], out.at[:, q_cols(t, h)], local_sem.at[heads + 2 + h]
        )
        mine.start()
        finished.append([mine])
        for i in range(1, n_tensor):
            their_rows = pl.ds(pl.multiple_of(tensor_at(i) * rows, rows), rows)
            c = remote(
                done.at[h, their_rows, :],
                out.at[:, q_cols(t, h)],
                ox_send.at[h, i],
                ox_recv.at[h, i],
                (p, tensor_at(i)),
            )
            c.start()
            finished[h].append(c)

    for h in range(heads):
        for c in exchange[h] + forward[h] + back[h]:
            c.wait_send()
        for c in finished[h]:
            c.wait()
    for c in exchange_kv:
        c.wait_send()


def on_device(
    n_pool, n_tensor, queries, incoming_keys, incoming_values, k_pages, v_pages, page_table, lengths
):
    slots, page, cols = k_pages.shape
    heads = cols // HEAD_SIZE
    rows = queries.shape[0]
    tokens = rows * n_tensor
    holder = lax.axis_index("pool")
    owners = (holder - jnp.arange(SPAN, dtype=jnp.int32)) % n_pool
    table_rows = jnp.take(page_table, owners, axis=0)
    global_slot = holder * slots + jnp.arange(slots, dtype=jnp.int32)
    matches = table_rows[:, :, None] == global_slot[None, None, :]
    page_index = jnp.arange(table_rows.shape[1], dtype=jnp.int32)[None, :, None]
    seen = jnp.sum(
        jnp.where(matches, jnp.take(lengths, owners)[:, None, None] - page_index * page, 0), axis=1
    )
    distance = jnp.sum(
        jnp.where(jnp.any(matches, axis=1), jnp.arange(SPAN, dtype=jnp.int32)[:, None], 0), axis=0
    )
    visible = jnp.arange(page, dtype=jnp.int32)[None, None, :] < seen[:, :, None]
    mask = visible.reshape(SPAN, slots * page).astype(jnp.bfloat16)
    mask_rows = jnp.concatenate([mask, jnp.zeros((16 - SPAN, slots * page), jnp.bfloat16)], axis=0)
    mask_each = jnp.broadcast_to(mask[:, None, :], (SPAN, 16, slots * page))

    vmem = pl.BlockSpec(memory_space=pltpu.VMEM)
    anywhere = pl.BlockSpec(memory_space=pl.ANY)
    dma = pltpu.SemaphoreType.DMA
    n_rows = GROUP * tokens
    bf16, f32 = jnp.bfloat16, jnp.float32
    scratch = [pltpu.VMEM((SPAN, tokens, WIDE), bf16) for _ in range(heads)] + [
        pltpu.VMEM((tokens, cols), bf16),
        pltpu.VMEM((tokens, cols), bf16),
        pltpu.VMEM((heads, slots, page, HEAD_SIZE), bf16),
        pltpu.VMEM((heads, slots, page, HEAD_SIZE), bf16),
        pltpu.VMEM((n_rows, slots * page), bf16),
        pltpu.VMEM((heads, n_rows, HEAD_SIZE), f32),
        pltpu.VMEM((heads, 16, n_rows), f32),
        pltpu.VMEM((heads, SPAN - 1, tokens, WIDE), bf16),
        pltpu.VMEM((heads, 16, n_rows), f32),
        pltpu.VMEM((heads, SPAN - 1, tokens, WIDE), bf16),
        pltpu.VMEM((heads, SPAN - 1, 16, n_rows), f32),
        pltpu.VMEM((heads, tokens, WIDE), bf16),
        dma((heads, 2)),
        dma((2 * heads + 2,)),
        dma((heads, n_tensor)),
        dma((heads, n_tensor)),
        dma((2, n_tensor)),
        dma((2, n_tensor)),
        dma((heads, SPAN)),
        dma((heads, SPAN)),
        dma((heads, SPAN)),
        dma((heads, SPAN)),
        dma((heads, SPAN)),
        dma((heads, SPAN)),
        dma((heads, n_tensor)),
        dma((heads, n_tensor)),
    ]
    return pl.pallas_call(
        functools.partial(kernel, n_pool, n_tensor, heads),
        out_shape=jax.ShapeDtypeStruct(queries.shape, queries.dtype),
        in_specs=[pl.BlockSpec(memory_space=pltpu.SMEM), vmem, vmem] + [anywhere] * 5,
        out_specs=anywhere,
        scratch_shapes=scratch,
        cost_estimate=pl.CostEstimate(
            flops=12 * heads * n_rows * slots * page * HEAD_SIZE,
            bytes_accessed=4 * slots * page * cols,
            transcendentals=2 * heads * n_rows * slots * page,
        ),
        compiler_params=pltpu.CompilerParams(
            collective_id=0, has_side_effects=True, vmem_limit_bytes=48 * 1024 * 1024
        ),
    )(
        distance,
        mask_rows,
        mask_each,
        queries,
        incoming_keys,
        incoming_values,
        k_pages,
        v_pages,
    )


def solution(mesh):
    placed = (
        P(("pool", "tensor"), None),
        P(("pool", "tensor"), None),
        P(("pool", "tensor"), None),
        P("pool", None, "tensor"),
        P("pool", None, "tensor"),
        P(),
        P(),
    )
    return jax.shard_map(
        functools.partial(on_device, mesh.shape["pool"], mesh.shape["tensor"]),
        mesh=mesh,
        in_specs=placed,
        out_specs=P(("pool", "tensor"), None),
        check_vma=False,
    )
```

```python
import functools
import math

import jax
import jax.numpy as jnp
from jax import lax
from jax.experimental import pallas as pl
from jax.experimental.pallas import tpu as pltpu
from jax.sharding import PartitionSpec as P

QUERY_HEADS = 16
KEY_VALUE_HEADS = 8
HEAD_SIZE = 256
SPAN = 4
SOFTCAP = 50.0

GROUP = QUERY_HEADS // KEY_VALUE_HEADS
WIDE = GROUP * HEAD_SIZE
INNER = HEAD_SIZE ** (-0.5) / SOFTCAP
OUTER = SOFTCAP * math.log2(math.e)
MESH = pl.DeviceIdType.MESH


def rows_by_head(block):
    return jnp.concatenate(
        [block[:, g * HEAD_SIZE : (g + 1) * HEAD_SIZE] for g in range(GROUP)], axis=0
    )


def tokens_by_head(block):
    n = block.shape[0] // GROUP
    return jnp.concatenate([block[g * n : (g + 1) * n] for g in range(GROUP)], axis=1)


def weigh(query, key):
    dots = lax.dot_general(query, key, (((1,), (1,)), ((), ())), preferred_element_type=jnp.float32)
    return jnp.exp2(OUTER * jnp.tanh(dots * INNER))


def kernel(
    n_pool,
    n_tensor,
    heads,
    dist,
    mask_rows,
    mask_each,
    q_in,
    k_in,
    v_in,
    k_pages,
    v_pages,
    out,
    *scratch,
):
    qbufs = scratch[:heads]
    (
        k_own,
        v_own,
        k_mem,
        v_mem,
        weights,
        own_numer,
        own_total,
        numer_out,
        total_out,
        numer_in,
        total_in,
        kept_numer,
        relay_in,
        done,
        page_sem,
        local_sem,
        qx_send,
        qx_recv,
        kx_send,
        kx_recv,
        qf_send,
        qf_recv,
        nr_send,
        nr_recv,
        tr_send,
        tr_recv,
        ox_send,
        ox_recv,
    ) = scratch[heads:]
    p = lax.axis_index("pool")
    t = lax.axis_index("tensor")
    rows = q_in.shape[0]
    tokens = rows * n_tensor
    slots = k_pages.shape[0]
    page = k_pages.shape[1]
    span_cols = heads * HEAD_SIZE

    def pool_at(d):
        return (lax.rem(p + d + n_pool, n_pool), t)

    def tensor_at(i):
        return lax.rem(t + i, n_tensor)

    page_copies = []
    for h in range(heads):
        cols = slice(h * HEAD_SIZE, (h + 1) * HEAD_SIZE)
        page_copies.append(
            [
                pltpu.make_async_copy(k_pages.at[:, :, cols], k_mem.at[h], page_sem.at[h, 0]),
                pltpu.make_async_copy(v_pages.at[:, :, cols], v_mem.at[h], page_sem.at[h, 1]),
            ]
        )

    my_rows = pl.ds(pl.multiple_of(t * rows, rows), rows)

    def q_cols(owner, h):
        return pl.ds(pl.multiple_of((owner * heads + h) * WIDE, WIDE), WIDE)

    local = []
    for h in range(heads):
        local.append(
            pltpu.make_async_copy(
                q_in.at[:, q_cols(t, h)], qbufs[h].at[0, my_rows, :], local_sem.at[h]
            )
        )
    own_cols = pl.ds(pl.multiple_of(t * span_cols, span_cols), span_cols)
    local_kv = [
        pltpu.make_async_copy(k_in.at[:, own_cols], k_own.at[my_rows, :], local_sem.at[heads]),
        pltpu.make_async_copy(v_in.at[:, own_cols], v_own.at[my_rows, :], local_sem.at[heads + 1]),
    ]
    for c in local:
        c.start()
    for c in page_copies[0]:
        c.start()

    barrier = pltpu.get_barrier_semaphore()
    for i in range(1, n_tensor):
        pl.semaphore_signal(barrier, inc=1, device_id=(p, tensor_at(i)), device_id_type=MESH)
    for d in range(1, SPAN):
        pl.semaphore_signal(barrier, inc=1, device_id=pool_at(d), device_id_type=MESH)
        pl.semaphore_signal(barrier, inc=1, device_id=pool_at(-d), device_id_type=MESH)
    pl.semaphore_wait(barrier, n_tensor - 1 + 2 * (SPAN - 1))

    def remote(src, dst, send, recv, device):
        return pltpu.make_async_remote_copy(
            src_ref=src,
            dst_ref=dst,
            send_sem=send,
            recv_sem=recv,
            device_id=device,
            device_id_type=MESH,
        )

    exchange = []
    for h in range(heads):
        exchange.append(
            [
                remote(
                    q_in.at[:, q_cols(tensor_at(i), h)],
                    qbufs[h].at[0, my_rows, :],
                    qx_send.at[h, i],
                    qx_recv.at[h, i],
                    (p, tensor_at(i)),
                )
                for i in range(1, n_tensor)
            ]
        )
        for c in exchange[h]:
            c.start()
    exchange_kv = []
    for i in range(1, n_tensor):
        their_cols = pl.ds(pl.multiple_of(tensor_at(i) * span_cols, span_cols), span_cols)
        for j, (src, dst) in enumerate(((k_in, k_own), (v_in, v_own))):
            exchange_kv.append(
                remote(
                    src.at[:, their_cols],
                    dst.at[my_rows, :],
                    kx_send.at[j, i],
                    kx_recv.at[j, i],
                    (p, tensor_at(i)),
                )
            )
    for c in local_kv:
        c.start()
    for c in exchange_kv:
        c.start()
    for pair in page_copies[1:]:
        for c in pair:
            c.start()

    even = lax.rem(p, 2) == 0

    def pass_query(h, have, give, hop, sem):
        return remote(
            qbufs[h].at[have],
            qbufs[h].at[give],
            qf_send.at[h, sem],
            qf_recv.at[h, give],
            pool_at(hop),
        )

    for h in range(heads):
        local[h].wait()
        for c in exchange[h]:
            c.wait_recv()

        @pl.when(even)
        def _():
            pass_query(h, 0, 2, 2, 1).start()
            pass_query(h, 0, 1, 1, 0).start()

        @pl.when(jnp.logical_not(even))
        def _():
            pass_query(h, 0, 1, 1, 0).start()
            pass_query(h, 0, 3, 3, 1).start()

    def send_numer(h, d, dst, recv, hop, sem):
        return remote(
            numer_out.at[h, d - 1], dst, nr_send.at[h, sem], nr_recv.at[h, recv], pool_at(hop)
        )

    def from_even(h):
        return [
            send_numer(h, 3, numer_in.at[h, 1], 1, -3, 0),
            send_numer(h, 1, numer_in.at[h, 0], 0, -1, 1),
            send_numer(h, 2, numer_in.at[h, 1], 1, -2, 2),
        ]

    def from_odd(h):
        return [
            send_numer(h, 1, numer_in.at[h, 0], 0, -1, 0),
            send_numer(h, 2, relay_in.at[h, 0], 2, -1, 1),
            send_numer(h, 3, relay_in.at[h, 1], 3, -1, 2),
        ]

    def combine(h):
        @pl.when(even)
        def _():
            for d in (1, 2):
                from_odd(h)[d].wait_recv()
                both = kept_numer[h, d - 1] + rows_by_head(relay_in[h, d - 1].astype(jnp.float32))
                numer_out[h, d - 1] = tokens_by_head(both.astype(jnp.bfloat16))
                from_even(h)[d].start()

    totals_back = []
    for h in range(heads):
        for c in page_copies[h]:
            c.wait()
        pass_query(h, 0, 1, 1, 0).wait_recv()

        @pl.when(even)
        def _():
            pass_query(h, 1, 2, 1, 2).start()

        pass_query(h, 0, 2, 2, 0).wait_recv()

        @pl.when(even)
        def _():
            pass_query(h, 2, 3, 1, 3).start()

        pass_query(h, 0, 3, 3, 0).wait_recv()

        qbuf = qbufs[h]

        @pl.loop(0, slots // 4)
        def _(j):
            for u in range(4):
                s = j * 4 + u
                query = rows_by_head(qbuf[dist[s]])
                cols = pl.ds(pl.multiple_of(s * page, page), page)
                weights[:, cols] = weigh(query, k_mem[h, s]).astype(jnp.bfloat16)

        values = v_mem[h].reshape(slots * page, HEAD_SIZE)
        totals = lax.dot_general(
            mask_rows[...],
            weights[...],
            (((1,), (1,)), ((), ())),
            preferred_element_type=jnp.float32,
        )[:8]
        own_total[h] = totals
        total_out[h] = totals
        totals_back.append([])
        for d in range(1, SPAN):
            c = remote(
                total_out.at[h],
                total_in.at[h, d - 1],
                tr_send.at[h, d],
                tr_recv.at[h, d],
                pool_at(-d),
            )
            c.start()
            totals_back[h].append(c)
        for d in (3, 2, 1, 0):
            all_weights = weights[...]
            kept = all_weights.reshape(-1, 16, slots * page) * mask_each[d][None]
            numer = jnp.dot(
                kept.reshape(all_weights.shape), values, preferred_element_type=jnp.float32
            )
            if d == 0:
                own_numer[h] = numer
                continue
            if d == 3:
                numer_out[h, d - 1] = tokens_by_head(numer.astype(jnp.bfloat16))

                @pl.when(even)
                def _():
                    from_even(h)[0].start()

            else:

                @pl.when(even)
                def _():
                    kept_numer[h, d - 1] = numer

                @pl.when(jnp.logical_not(even))
                def _():
                    numer_out[h, d - 1] = tokens_by_head(numer.astype(jnp.bfloat16))

            @pl.when(jnp.logical_not(even))
            def _():
                from_odd(h)[d - 1].start()

        if h > 0:
            combine(h - 1)

    for c in local_kv:
        c.wait()
    for c in exchange_kv:
        c.wait_recv()
    n_rows = GROUP * tokens
    query_token = lax.broadcasted_iota(jnp.int32, (n_rows, tokens), 0) % tokens
    causal = lax.broadcasted_iota(jnp.int32, (n_rows, tokens), 1) <= query_token
    ones = jnp.ones((16, tokens), jnp.bfloat16)
    for h in range(heads):
        cols = slice(h * HEAD_SIZE, (h + 1) * HEAD_SIZE)
        fresh = jnp.where(causal, weigh(rows_by_head(qbufs[h][0]), k_own[:, cols]), 0.0)
        fresh = fresh.astype(jnp.bfloat16)
        own_numer[h] += jnp.dot(fresh, v_own[:, cols], preferred_element_type=jnp.float32)
        own_total[h] += lax.dot_general(
            ones, fresh, (((1,), (1,)), ((), ())), preferred_element_type=jnp.float32
        )[:8]

    combine(heads - 1)

    finished = []
    for h in range(heads):
        for c in totals_back[h]:
            c.wait_recv()
        send_numer(h, 1, numer_in.at[h, 0], 0, -1, 0).wait_recv()
        send_numer(h, 1, numer_in.at[h, 1], 1, -2, 0).wait_recv()
        total = own_total[h, 0:1, :]
        numer = own_numer[h]
        for d in range(1, SPAN):
            total = total + total_in[h, d - 1, d : d + 1, :]
        for d in range(2):
            numer = numer + rows_by_head(numer_in[h, d].astype(jnp.float32))
        per_row = jnp.broadcast_to(total, (128, n_rows)).T
        per_row = jnp.concatenate([per_row] * (HEAD_SIZE // 128), axis=1)
        done[h] = tokens_by_head((numer / per_row).astype(jnp.bfloat16))
        mine = pltpu.make_async_copy(
            done.at[h, my_rows, :], out.at[:, q_cols(t, h)], local_sem.at[heads + 2 + h]
        )
        mine.start()
        finished.append([mine])
        for i in range(1, n_tensor):
            their_rows = pl.ds(pl.multiple_of(tensor_at(i) * rows, rows), rows)
            c = remote(
                done.at[h, their_rows, :],
                out.at[:, q_cols(t, h)],
                ox_send.at[h, i],
                ox_recv.at[h, i],
                (p, tensor_at(i)),
            )
            c.start()
            finished[h].append(c)

    for h in range(heads):
        for c in exchange[h] + totals_back[h]:
            c.wait_send()

        @pl.when(even)
        def _():
            pass_query(h, 0, 1, 1, 0).wait_send()
            pass_query(h, 0, 2, 2, 1).wait_send()
            pass_query(h, 1, 2, 1, 2).wait_send()
            pass_query(h, 2, 3, 1, 3).wait_send()
            for c in from_even(h):
                c.wait_send()

        @pl.when(jnp.logical_not(even))
        def _():
            pass_query(h, 0, 1, 1, 0).wait_send()
            pass_query(h, 0, 3, 3, 1).wait_send()
            for c in from_odd(h):
                c.wait_send()

        for c in finished[h]:
            c.wait()
    for c in exchange_kv:
        c.wait_send()


def on_device(
    n_pool, n_tensor, queries, incoming_keys, incoming_values, k_pages, v_pages, page_table, lengths
):
    slots, page, cols = k_pages.shape
    heads = cols // HEAD_SIZE
    rows = queries.shape[0]
    tokens = rows * n_tensor
    holder = lax.axis_index("pool")
    first = holder - (SPAN - 1) + n_pool

    def of_owners(whole):
        twice = jnp.concatenate([whole, whole], axis=0)
        return lax.dynamic_slice_in_dim(twice, first, SPAN, axis=0)[::-1]

    table_rows = of_owners(page_table)
    global_slot = holder * slots + jnp.arange(slots, dtype=jnp.int32)
    matches = table_rows[:, :, None] == global_slot[None, None, :]
    page_index = jnp.arange(table_rows.shape[1], dtype=jnp.int32)[None, :, None]
    seen = jnp.sum(
        jnp.where(matches, of_owners(lengths)[:, None, None] - page_index * page, 0), axis=1
    )
    distance = jnp.sum(
        jnp.where(jnp.any(matches, axis=1), jnp.arange(SPAN, dtype=jnp.int32)[:, None], 0), axis=0
    )
    visible = jnp.arange(page, dtype=jnp.int32)[None, None, :] < seen[:, :, None]
    mask = visible.reshape(SPAN, slots * page).astype(jnp.bfloat16)
    mask_rows = jnp.concatenate([mask, jnp.zeros((16 - SPAN, slots * page), jnp.bfloat16)], axis=0)
    mask_each = jnp.broadcast_to(mask[:, None, :], (SPAN, 16, slots * page))

    vmem = pl.BlockSpec(memory_space=pltpu.VMEM)
    anywhere = pl.BlockSpec(memory_space=pltpu.HBM)
    dma = pltpu.SemaphoreType.DMA
    n_rows = GROUP * tokens
    bf16, f32 = jnp.bfloat16, jnp.float32
    scratch = [pltpu.VMEM((SPAN, tokens, WIDE), bf16) for _ in range(heads)] + [
        pltpu.VMEM((tokens, cols), bf16),
        pltpu.VMEM((tokens, cols), bf16),
        pltpu.VMEM((heads, slots, page, HEAD_SIZE), bf16),
        pltpu.VMEM((heads, slots, page, HEAD_SIZE), bf16),
        pltpu.VMEM((n_rows, slots * page), bf16),
        pltpu.VMEM((heads, n_rows, HEAD_SIZE), f32),
        pltpu.VMEM((heads, 8, n_rows), f32),
        pltpu.VMEM((heads, SPAN - 1, tokens, WIDE), bf16),
        pltpu.VMEM((heads, 8, n_rows), f32),
        pltpu.VMEM((heads, 2, tokens, WIDE), bf16),
        pltpu.VMEM((heads, SPAN - 1, 8, n_rows), f32),
        pltpu.VMEM((heads, 2, n_rows, HEAD_SIZE), f32),
        pltpu.VMEM((heads, 2, tokens, WIDE), bf16),
        pltpu.VMEM((heads, tokens, WIDE), bf16),
        dma((heads, 2)),
        dma((2 * heads + 2,)),
        dma((heads, n_tensor)),
        dma((heads, n_tensor)),
        dma((2, n_tensor)),
        dma((2, n_tensor)),
        dma((heads, SPAN)),
        dma((heads, SPAN)),
        dma((heads, SPAN)),
        dma((heads, SPAN)),
        dma((heads, SPAN)),
        dma((heads, SPAN)),
        dma((heads, n_tensor)),
        dma((heads, n_tensor)),
    ]
    return pl.pallas_call(
        functools.partial(kernel, n_pool, n_tensor, heads),
        out_shape=jax.ShapeDtypeStruct(queries.shape, queries.dtype),
        in_specs=[pl.BlockSpec(memory_space=pltpu.SMEM), vmem, vmem] + [anywhere] * 5,
        out_specs=anywhere,
        scratch_shapes=scratch,
        cost_estimate=pl.CostEstimate(
            flops=12 * heads * n_rows * slots * page * HEAD_SIZE,
            bytes_accessed=4 * slots * page * cols,
            transcendentals=2 * heads * n_rows * slots * page,
        ),
        compiler_params=pltpu.CompilerParams(
            collective_id=0, has_side_effects=True, vmem_limit_bytes=62 * 1024 * 1024
        ),
    )(
        distance,
        mask_rows,
        mask_each,
        queries,
        incoming_keys,
        incoming_values,
        k_pages,
        v_pages,
    )


def solution(mesh):
    placed = (
        P(("pool", "tensor"), None),
        P(("pool", "tensor"), None),
        P(("pool", "tensor"), None),
        P("pool", None, "tensor"),
        P("pool", None, "tensor"),
        P(),
        P(),
    )
    return jax.shard_map(
        functools.partial(on_device, mesh.shape["pool"], mesh.shape["tensor"]),
        mesh=mesh,
        in_specs=placed,
        out_specs=P(("pool", "tensor"), None),
        check_vma=False,
    )
```

```python
import functools
import math

import jax
import jax.numpy as jnp
from jax import lax
from jax.experimental import pallas as pl
from jax.experimental.pallas import tpu as pltpu
from jax.sharding import PartitionSpec as P

QUERY_HEADS = 16
KEY_VALUE_HEADS = 8
HEAD_SIZE = 256
SPAN = 4
SOFTCAP = 50.0

GROUP = QUERY_HEADS // KEY_VALUE_HEADS
WIDE = GROUP * HEAD_SIZE
INNER = HEAD_SIZE ** (-0.5) / SOFTCAP
OUTER = SOFTCAP * math.log2(math.e)
MESH = pl.DeviceIdType.MESH


def rows_by_head(block):
    return jnp.concatenate(
        [block[:, g * HEAD_SIZE : (g + 1) * HEAD_SIZE] for g in range(GROUP)], axis=0
    )


def tokens_by_head(block):
    n = block.shape[0] // GROUP
    return jnp.concatenate([block[g * n : (g + 1) * n] for g in range(GROUP)], axis=1)


def weigh(query, key):
    dots = lax.dot_general(query, key, (((1,), (1,)), ((), ())), preferred_element_type=jnp.float32)
    return jnp.exp2(OUTER * jnp.tanh(dots * INNER))


def kernel(
    n_pool,
    n_tensor,
    heads,
    seen_all,
    q_in,
    k_in,
    v_in,
    k_pages,
    v_pages,
    out,
    *scratch,
):
    qbufs = scratch[:heads]
    (
        mask_rows,
        mask_each,
        k_own,
        v_own,
        k_mem,
        v_mem,
        weights,
        own_numer,
        own_total,
        numer_out,
        total_out,
        numer_in,
        total_in,
        kept_numer,
        relay_in,
        done,
        page_sem,
        local_sem,
        qx_send,
        qx_recv,
        kx_send,
        kx_recv,
        qf_send,
        qf_recv,
        nr_send,
        nr_recv,
        tr_send,
        tr_recv,
        ox_send,
        ox_recv,
    ) = scratch[heads:]
    p = lax.axis_index("pool")
    t = lax.axis_index("tensor")
    rows = q_in.shape[0]
    tokens = rows * n_tensor
    slots = k_pages.shape[0]
    page = k_pages.shape[1]
    span_cols = heads * HEAD_SIZE

    def pool_at(d):
        return (lax.rem(p + d + n_pool, n_pool), t)

    def tensor_at(i):
        return lax.rem(t + i, n_tensor)

    page_copies = []
    for h in range(heads):
        cols = slice(h * HEAD_SIZE, (h + 1) * HEAD_SIZE)
        page_copies.append(
            [
                pltpu.make_async_copy(k_pages.at[:, :, cols], k_mem.at[h], page_sem.at[h, 0]),
                pltpu.make_async_copy(v_pages.at[:, :, cols], v_mem.at[h], page_sem.at[h, 1]),
            ]
        )

    my_rows = pl.ds(pl.multiple_of(t * rows, rows), rows)

    def q_cols(owner, h):
        return pl.ds(pl.multiple_of((owner * heads + h) * WIDE, WIDE), WIDE)

    local = []
    for h in range(heads):
        local.append(
            pltpu.make_async_copy(
                q_in.at[:, q_cols(t, h)], qbufs[h].at[0, my_rows, :], local_sem.at[h]
            )
        )
    own_cols = pl.ds(pl.multiple_of(t * span_cols, span_cols), span_cols)
    local_kv = [
        pltpu.make_async_copy(k_in.at[:, own_cols], k_own.at[my_rows, :], local_sem.at[heads]),
        pltpu.make_async_copy(v_in.at[:, own_cols], v_own.at[my_rows, :], local_sem.at[heads + 1]),
    ]
    for c in local:
        c.start()
    for c in page_copies[0]:
        c.start()

    barrier = pltpu.get_barrier_semaphore()
    for i in range(1, n_tensor):
        pl.semaphore_signal(barrier, inc=1, device_id=(p, tensor_at(i)), device_id_type=MESH)
    for d in range(1, SPAN):
        pl.semaphore_signal(barrier, inc=1, device_id=pool_at(d), device_id_type=MESH)
        pl.semaphore_signal(barrier, inc=1, device_id=pool_at(-d), device_id_type=MESH)
    pl.semaphore_wait(barrier, n_tensor - 1 + 2 * (SPAN - 1))

    def remote(src, dst, send, recv, device):
        return pltpu.make_async_remote_copy(
            src_ref=src,
            dst_ref=dst,
            send_sem=send,
            recv_sem=recv,
            device_id=device,
            device_id_type=MESH,
        )

    exchange = []
    for h in range(heads):
        exchange.append(
            [
                remote(
                    q_in.at[:, q_cols(tensor_at(i), h)],
                    qbufs[h].at[0, my_rows, :],
                    qx_send.at[h, i],
                    qx_recv.at[h, i],
                    (p, tensor_at(i)),
                )
                for i in range(1, n_tensor)
            ]
        )
        for c in exchange[h]:
            c.start()
    exchange_kv = []
    for i in range(1, n_tensor):
        their_cols = pl.ds(pl.multiple_of(tensor_at(i) * span_cols, span_cols), span_cols)
        for j, (src, dst) in enumerate(((k_in, k_own), (v_in, v_own))):
            exchange_kv.append(
                remote(
                    src.at[:, their_cols],
                    dst.at[my_rows, :],
                    kx_send.at[j, i],
                    kx_recv.at[j, i],
                    (p, tensor_at(i)),
                )
            )
    for c in local_kv:
        c.start()
    for c in exchange_kv:
        c.start()
    for pair in page_copies[1:]:
        for c in pair:
            c.start()

    even = lax.rem(p, 2) == 0

    def pass_query(h, have, give, hop, sem):
        return remote(
            qbufs[h].at[have],
            qbufs[h].at[give],
            qf_send.at[h, sem],
            qf_recv.at[h, give],
            pool_at(hop),
        )

    for h in range(heads):
        local[h].wait()
        for c in exchange[h]:
            c.wait_recv()

        @pl.when(even)
        def _():
            pass_query(h, 0, 2, 2, 1).start()
            pass_query(h, 0, 1, 1, 0).start()

        @pl.when(jnp.logical_not(even))
        def _():
            pass_query(h, 0, 1, 1, 0).start()
            pass_query(h, 0, 3, 3, 1).start()

    def send_numer(h, d, dst, recv, hop, sem):
        return remote(
            numer_out.at[h, d - 1], dst, nr_send.at[h, sem], nr_recv.at[h, recv], pool_at(hop)
        )

    def from_even(h):
        return [
            send_numer(h, 3, numer_in.at[h, 1], 1, -3, 0),
            send_numer(h, 1, numer_in.at[h, 0], 0, -1, 1),
            send_numer(h, 2, numer_in.at[h, 1], 1, -2, 2),
        ]

    def from_odd(h):
        return [
            send_numer(h, 1, numer_in.at[h, 0], 0, -1, 0),
            send_numer(h, 2, relay_in.at[h, 0], 2, -1, 1),
            send_numer(h, 3, relay_in.at[h, 1], 3, -1, 2),
        ]

    def combine(h):
        @pl.when(even)
        def _():
            for d in (1, 2):
                from_odd(h)[d].wait_recv()
                both = kept_numer[h, d - 1] + rows_by_head(relay_in[h, d - 1].astype(jnp.float32))
                numer_out[h, d - 1] = tokens_by_head(both.astype(jnp.bfloat16))
                from_even(h)[d].start()

    seen = [[seen_all[lax.rem(p - d + n_pool, n_pool), s] for s in range(slots)] for d in range(SPAN)]
    dist = [
        sum(jnp.where(seen[d][s] > 0, d, 0).astype(jnp.int32) for d in range(1, SPAN))
        for s in range(slots)
    ]
    tile = (16, page)
    column = lax.broadcasted_iota(jnp.int32, tile, 1)
    row = lax.broadcasted_iota(jnp.int32, tile, 0)
    for s in range(slots):
        cols = slice(s * page, (s + 1) * page)
        by_row = jnp.zeros(tile, jnp.int32)
        for d in range(SPAN):
            mask_each[d, :, cols] = jnp.where(column < seen[d][s], 1.0, 0.0).astype(jnp.bfloat16)
            by_row = jnp.where(row == d, seen[d][s], by_row)
        mask_rows[:, cols] = jnp.where(column < by_row, 1.0, 0.0).astype(jnp.bfloat16)

    totals_back = []
    for h in range(heads):
        for c in page_copies[h]:
            c.wait()
        pass_query(h, 0, 1, 1, 0).wait_recv()

        @pl.when(even)
        def _():
            pass_query(h, 1, 2, 1, 2).start()

        pass_query(h, 0, 2, 2, 0).wait_recv()

        @pl.when(even)
        def _():
            pass_query(h, 2, 3, 1, 3).start()

        pass_query(h, 0, 3, 3, 0).wait_recv()

        qbuf = qbufs[h]

        for s in range(slots):
            query = rows_by_head(qbuf[dist[s]])
            cols = slice(s * page, (s + 1) * page)
            weights[:, cols] = weigh(query, k_mem[h, s]).astype(jnp.bfloat16)

        values = v_mem[h].reshape(slots * page, HEAD_SIZE)
        totals = lax.dot_general(
            mask_rows[...],
            weights[...],
            (((1,), (1,)), ((), ())),
            preferred_element_type=jnp.float32,
        )[:8]
        own_total[h] = totals
        total_out[h] = totals
        totals_back.append([])
        for d in range(1, SPAN):
            c = remote(
                total_out.at[h],
                total_in.at[h, d - 1],
                tr_send.at[h, d],
                tr_recv.at[h, d],
                pool_at(-d),
            )
            c.start()
            totals_back[h].append(c)
        for d in (3, 2, 1, 0):
            all_weights = weights[...]
            kept = all_weights.reshape(-1, 16, slots * page) * mask_each[d][None]
            numer = jnp.dot(
                kept.reshape(all_weights.shape), values, preferred_element_type=jnp.float32
            )
            if d == 0:
                own_numer[h] = numer
                continue
            if d == 3:
                numer_out[h, d - 1] = tokens_by_head(numer.astype(jnp.bfloat16))

                @pl.when(even)
                def _():
                    from_even(h)[0].start()

            else:

                @pl.when(even)
                def _():
                    kept_numer[h, d - 1] = numer

                @pl.when(jnp.logical_not(even))
                def _():
                    numer_out[h, d - 1] = tokens_by_head(numer.astype(jnp.bfloat16))

            @pl.when(jnp.logical_not(even))
            def _():
                from_odd(h)[d - 1].start()

        if h > 0:
            combine(h - 1)

    for c in local_kv:
        c.wait()
    for c in exchange_kv:
        c.wait_recv()
    n_rows = GROUP * tokens
    query_token = lax.broadcasted_iota(jnp.int32, (n_rows, tokens), 0) % tokens
    causal = lax.broadcasted_iota(jnp.int32, (n_rows, tokens), 1) <= query_token
    ones = jnp.ones((16, tokens), jnp.bfloat16)
    for h in range(heads):
        cols = slice(h * HEAD_SIZE, (h + 1) * HEAD_SIZE)
        fresh = jnp.where(causal, weigh(rows_by_head(qbufs[h][0]), k_own[:, cols]), 0.0)
        fresh = fresh.astype(jnp.bfloat16)
        own_numer[h] += jnp.dot(fresh, v_own[:, cols], preferred_element_type=jnp.float32)
        own_total[h] += lax.dot_general(
            ones, fresh, (((1,), (1,)), ((), ())), preferred_element_type=jnp.float32
        )[:8]

    combine(heads - 1)

    finished = []
    for h in range(heads):
        for c in totals_back[h]:
            c.wait_recv()
        send_numer(h, 1, numer_in.at[h, 0], 0, -1, 0).wait_recv()
        send_numer(h, 1, numer_in.at[h, 1], 1, -2, 0).wait_recv()
        total = own_total[h, 0:1, :]
        numer = own_numer[h]
        for d in range(1, SPAN):
            total = total + total_in[h, d - 1, d : d + 1, :]
        for d in range(2):
            numer = numer + rows_by_head(numer_in[h, d].astype(jnp.float32))
        per_row = jnp.broadcast_to(total, (128, n_rows)).T
        per_row = jnp.concatenate([per_row] * (HEAD_SIZE // 128), axis=1)
        done[h] = tokens_by_head((numer / per_row).astype(jnp.bfloat16))
        mine = pltpu.make_async_copy(
            done.at[h, my_rows, :], out.at[:, q_cols(t, h)], local_sem.at[heads + 2 + h]
        )
        mine.start()
        finished.append([mine])
        for i in range(1, n_tensor):
            their_rows = pl.ds(pl.multiple_of(tensor_at(i) * rows, rows), rows)
            c = remote(
                done.at[h, their_rows, :],
                out.at[:, q_cols(t, h)],
                ox_send.at[h, i],
                ox_recv.at[h, i],
                (p, tensor_at(i)),
            )
            c.start()
            finished[h].append(c)

    for h in range(heads):
        for c in exchange[h] + totals_back[h]:
            c.wait_send()

        @pl.when(even)
        def _():
            pass_query(h, 0, 1, 1, 0).wait_send()
            pass_query(h, 0, 2, 2, 1).wait_send()
            pass_query(h, 1, 2, 1, 2).wait_send()
            pass_query(h, 2, 3, 1, 3).wait_send()
            for c in from_even(h):
                c.wait_send()

        @pl.when(jnp.logical_not(even))
        def _():
            pass_query(h, 0, 1, 1, 0).wait_send()
            pass_query(h, 0, 3, 3, 1).wait_send()
            for c in from_odd(h):
                c.wait_send()

        for c in finished[h]:
            c.wait()
    for c in exchange_kv:
        c.wait_send()


def on_device(
    n_pool, n_tensor, queries, incoming_keys, incoming_values, k_pages, v_pages, page_table, lengths
):
    slots, page, cols = k_pages.shape
    heads = cols // HEAD_SIZE
    rows = queries.shape[0]
    tokens = rows * n_tensor
    holder = lax.axis_index("pool")
    global_slot = holder * slots + jnp.arange(slots, dtype=jnp.int32)
    matches = page_table[:, :, None] == global_slot[None, None, :]
    page_index = jnp.arange(page_table.shape[1], dtype=jnp.int32)[None, :, None]
    seen_all = jnp.sum(jnp.where(matches, lengths[:, None, None] - page_index * page, 0), axis=1)

    anywhere = pl.BlockSpec(memory_space=pltpu.HBM)
    dma = pltpu.SemaphoreType.DMA
    n_rows = GROUP * tokens
    bf16, f32 = jnp.bfloat16, jnp.float32
    scratch = [pltpu.VMEM((SPAN, tokens, WIDE), bf16) for _ in range(heads)] + [
        pltpu.VMEM((16, slots * page), bf16),
        pltpu.VMEM((SPAN, 16, slots * page), bf16),
        pltpu.VMEM((tokens, cols), bf16),
        pltpu.VMEM((tokens, cols), bf16),
        pltpu.VMEM((heads, slots, page, HEAD_SIZE), bf16),
        pltpu.VMEM((heads, slots, page, HEAD_SIZE), bf16),
        pltpu.VMEM((n_rows, slots * page), bf16),
        pltpu.VMEM((heads, n_rows, HEAD_SIZE), f32),
        pltpu.VMEM((heads, 8, n_rows), f32),
        pltpu.VMEM((heads, SPAN - 1, tokens, WIDE), bf16),
        pltpu.VMEM((heads, 8, n_rows), f32),
        pltpu.VMEM((heads, 2, tokens, WIDE), bf16),
        pltpu.VMEM((heads, SPAN - 1, 8, n_rows), f32),
        pltpu.VMEM((heads, 2, n_rows, HEAD_SIZE), f32),
        pltpu.VMEM((heads, 2, tokens, WIDE), bf16),
        pltpu.VMEM((heads, tokens, WIDE), bf16),
        dma((heads, 2)),
        dma((2 * heads + 2,)),
        dma((heads, n_tensor)),
        dma((heads, n_tensor)),
        dma((2, n_tensor)),
        dma((2, n_tensor)),
        dma((heads, SPAN)),
        dma((heads, SPAN)),
        dma((heads, SPAN)),
        dma((heads, SPAN)),
        dma((heads, SPAN)),
        dma((heads, SPAN)),
        dma((heads, n_tensor)),
        dma((heads, n_tensor)),
    ]
    return pl.pallas_call(
        functools.partial(kernel, n_pool, n_tensor, heads),
        out_shape=jax.ShapeDtypeStruct(queries.shape, queries.dtype),
        in_specs=[pl.BlockSpec(memory_space=pltpu.SMEM)] + [anywhere] * 5,
        out_specs=pl.BlockSpec(memory_space=pl.ANY),
        scratch_shapes=scratch,
        cost_estimate=pl.CostEstimate(
            flops=12 * heads * n_rows * slots * page * HEAD_SIZE,
            bytes_accessed=4 * slots * page * cols,
            transcendentals=2 * heads * n_rows * slots * page,
        ),
        compiler_params=pltpu.CompilerParams(
            collective_id=0, has_side_effects=True, vmem_limit_bytes=62 * 1024 * 1024
        ),
    )(
        seen_all,
        queries,
        incoming_keys,
        incoming_values,
        k_pages,
        v_pages,
    )


def solution(mesh):
    placed = (
        P(("pool", "tensor"), None),
        P(("pool", "tensor"), None),
        P(("pool", "tensor"), None),
        P("pool", None, "tensor"),
        P("pool", None, "tensor"),
        P(),
        P(),
    )
    return jax.shard_map(
        functools.partial(on_device, mesh.shape["pool"], mesh.shape["tensor"]),
        mesh=mesh,
        in_specs=placed,
        out_specs=P(("pool", "tensor"), None),
        check_vma=False,
    )
```

```python
import functools
import math

import jax
import jax.numpy as jnp
from jax import lax
from jax.experimental import pallas as pl
from jax.experimental.pallas import tpu as pltpu
from jax.sharding import PartitionSpec as P

QUERY_HEADS = 16
KEY_VALUE_HEADS = 8
HEAD_SIZE = 256
SPAN = 4
SOFTCAP = 50.0

GROUP = QUERY_HEADS // KEY_VALUE_HEADS
WIDE = GROUP * HEAD_SIZE
INNER = HEAD_SIZE ** (-0.5) / SOFTCAP
OUTER = SOFTCAP * math.log2(math.e)
MESH = pl.DeviceIdType.MESH


def rows_by_head(block):
    return jnp.concatenate(
        [block[:, g * HEAD_SIZE : (g + 1) * HEAD_SIZE] for g in range(GROUP)], axis=0
    )


def tokens_by_head(block):
    n = block.shape[0] // GROUP
    return jnp.concatenate([block[g * n : (g + 1) * n] for g in range(GROUP)], axis=1)


def weigh(query, key):
    dots = lax.dot_general(query, key, (((1,), (1,)), ((), ())), preferred_element_type=jnp.float32)
    return jnp.exp2(OUTER * jnp.tanh(dots * INNER))


def kernel(
    n_pool,
    n_tensor,
    heads,
    seen_all,
    q_in,
    k_in,
    v_in,
    k_pages,
    v_pages,
    out,
    *scratch,
):
    qbufs = scratch[:heads]
    (
        mask_rows,
        mask_each,
        k_own,
        v_own,
        k_mem,
        v_mem,
        weights,
        own_numer,
        own_total,
        numer_out,
        total_out,
        numer_in,
        total_in,
        kept_numer,
        relay_in,
        done,
        page_sem,
        local_sem,
        qx_send,
        qx_recv,
        kx_send,
        kx_recv,
        qf_send,
        qf_recv,
        nr_send,
        nr_recv,
        tr_send,
        tr_recv,
        ox_send,
        ox_recv,
    ) = scratch[heads:]
    p = lax.axis_index("pool")
    t = lax.axis_index("tensor")
    rows = q_in.shape[0]
    tokens = rows * n_tensor
    slots = k_pages.shape[0]
    page = k_pages.shape[1]
    span_cols = heads * HEAD_SIZE

    def pool_at(d):
        return (lax.rem(p + d + n_pool, n_pool), t)

    def tensor_at(i):
        return lax.rem(t + i, n_tensor)

    page_copies = []
    for h in range(heads):
        cols = slice(h * HEAD_SIZE, (h + 1) * HEAD_SIZE)
        page_copies.append(
            [
                pltpu.make_async_copy(k_pages.at[:, :, cols], k_mem.at[h], page_sem.at[h, 0]),
                pltpu.make_async_copy(v_pages.at[:, :, cols], v_mem.at[h], page_sem.at[h, 1]),
            ]
        )

    my_rows = pl.ds(pl.multiple_of(t * rows, rows), rows)

    def q_cols(owner, h):
        return pl.ds(pl.multiple_of((owner * heads + h) * WIDE, WIDE), WIDE)

    local = []
    for h in range(heads):
        local.append(
            pltpu.make_async_copy(
                q_in.at[:, q_cols(t, h)], qbufs[h].at[0, my_rows, :], local_sem.at[h]
            )
        )
    own_cols = pl.ds(pl.multiple_of(t * span_cols, span_cols), span_cols)
    local_kv = [
        pltpu.make_async_copy(k_in.at[:, own_cols], k_own.at[my_rows, :], local_sem.at[heads]),
        pltpu.make_async_copy(v_in.at[:, own_cols], v_own.at[my_rows, :], local_sem.at[heads + 1]),
    ]
    for c in local:
        c.start()
    for c in page_copies[0]:
        c.start()

    barrier = pltpu.get_barrier_semaphore()
    for i in range(1, n_tensor):
        pl.semaphore_signal(barrier, inc=1, device_id=(p, tensor_at(i)), device_id_type=MESH)
    for d in range(1, SPAN):
        pl.semaphore_signal(barrier, inc=1, device_id=pool_at(d), device_id_type=MESH)
        pl.semaphore_signal(barrier, inc=1, device_id=pool_at(-d), device_id_type=MESH)
    pl.semaphore_wait(barrier, n_tensor - 1 + 2 * (SPAN - 1))

    def remote(src, dst, send, recv, device):
        return pltpu.make_async_remote_copy(
            src_ref=src,
            dst_ref=dst,
            send_sem=send,
            recv_sem=recv,
            device_id=device,
            device_id_type=MESH,
        )

    exchange = []
    for h in range(heads):
        exchange.append(
            [
                remote(
                    q_in.at[:, q_cols(tensor_at(i), h)],
                    qbufs[h].at[0, my_rows, :],
                    qx_send.at[h, i],
                    qx_recv.at[h, i],
                    (p, tensor_at(i)),
                )
                for i in range(1, n_tensor)
            ]
        )
        for c in exchange[h]:
            c.start()
    exchange_kv = []
    for i in range(1, n_tensor):
        their_cols = pl.ds(pl.multiple_of(tensor_at(i) * span_cols, span_cols), span_cols)
        for j, (src, dst) in enumerate(((k_in, k_own), (v_in, v_own))):
            exchange_kv.append(
                remote(
                    src.at[:, their_cols],
                    dst.at[my_rows, :],
                    kx_send.at[j, i],
                    kx_recv.at[j, i],
                    (p, tensor_at(i)),
                )
            )
    for pair in page_copies[1:]:
        for c in pair:
            c.start()

    even = lax.rem(p, 2) == 0

    def pass_query(h, have, give, hop, sem):
        return remote(
            qbufs[h].at[have],
            qbufs[h].at[give],
            qf_send.at[h, sem],
            qf_recv.at[h, give],
            pool_at(hop),
        )

    for h in range(heads):
        local[h].wait()
        for c in exchange[h]:
            c.wait_recv()

        @pl.when(even)
        def _():
            pass_query(h, 0, 2, 2, 1).start()
            pass_query(h, 0, 1, 1, 0).start()

        @pl.when(jnp.logical_not(even))
        def _():
            pass_query(h, 0, 1, 1, 0).start()
            pass_query(h, 0, 3, 3, 1).start()

    for c in local_kv:
        c.start()
    for c in exchange_kv:
        c.start()

    def send_numer(h, d, dst, recv, hop, sem):
        return remote(
            numer_out.at[h, d - 1], dst, nr_send.at[h, sem], nr_recv.at[h, recv], pool_at(hop)
        )

    def from_even(h):
        return [
            send_numer(h, 3, numer_in.at[h, 1], 1, -3, 0),
            send_numer(h, 1, numer_in.at[h, 0], 0, -1, 1),
            send_numer(h, 2, numer_in.at[h, 1], 1, -2, 2),
        ]

    def from_odd(h):
        return [
            send_numer(h, 1, numer_in.at[h, 0], 0, -1, 0),
            send_numer(h, 2, relay_in.at[h, 0], 2, -1, 1),
            send_numer(h, 3, relay_in.at[h, 1], 3, -1, 2),
        ]

    def combine(h):
        @pl.when(even)
        def _():
            for d in (1, 2):
                from_odd(h)[d].wait_recv()
                both = kept_numer[h, d - 1] + rows_by_head(relay_in[h, d - 1].astype(jnp.float32))
                numer_out[h, d - 1] = tokens_by_head(both.astype(jnp.bfloat16))
                from_even(h)[d].start()

    seen = [[seen_all[lax.rem(p - d + n_pool, n_pool), s] for s in range(slots)] for d in range(SPAN)]
    dist = [
        sum(jnp.where(seen[d][s] > 0, d, 0).astype(jnp.int32) for d in range(1, SPAN))
        for s in range(slots)
    ]
    tile = (16, page)
    column = lax.broadcasted_iota(jnp.int32, tile, 1)
    row = lax.broadcasted_iota(jnp.int32, tile, 0)
    for s in range(slots):
        cols = slice(s * page, (s + 1) * page)
        by_row = jnp.zeros(tile, jnp.int32)
        for d in range(SPAN):
            mask_each[d, :, cols] = jnp.where(column < seen[d][s], 1.0, 0.0).astype(jnp.bfloat16)
            by_row = jnp.where(row == d, seen[d][s], by_row)
        mask_rows[:, cols] = jnp.where(column < by_row, 1.0, 0.0).astype(jnp.bfloat16)

    totals_back = []
    for h in range(heads):
        for c in page_copies[h]:
            c.wait()
        pass_query(h, 0, 1, 1, 0).wait_recv()

        @pl.when(even)
        def _():
            pass_query(h, 1, 2, 1, 2).start()

        pass_query(h, 0, 2, 2, 0).wait_recv()

        @pl.when(even)
        def _():
            pass_query(h, 2, 3, 1, 3).start()

        pass_query(h, 0, 3, 3, 0).wait_recv()

        qbuf = qbufs[h]

        for s in range(slots):
            query = rows_by_head(qbuf[dist[s]])
            cols = slice(s * page, (s + 1) * page)
            weights[:, cols] = weigh(query, k_mem[h, s]).astype(jnp.bfloat16)

        values = v_mem[h].reshape(slots * page, HEAD_SIZE)
        totals = lax.dot_general(
            mask_rows[...],
            weights[...],
            (((1,), (1,)), ((), ())),
            preferred_element_type=jnp.float32,
        )[:8]
        own_total[h] = totals
        total_out[h] = totals
        totals_back.append([])
        for d in range(1, SPAN):
            c = remote(
                total_out.at[h],
                total_in.at[h, d - 1],
                tr_send.at[h, d],
                tr_recv.at[h, d],
                pool_at(-d),
            )
            c.start()
            totals_back[h].append(c)
        for d in (3, 2, 1, 0):
            all_weights = weights[...]
            kept = all_weights.reshape(-1, 16, slots * page) * mask_each[d][None]
            numer = jnp.dot(
                kept.reshape(all_weights.shape), values, preferred_element_type=jnp.float32
            )
            if d == 0:
                own_numer[h] = numer
                continue
            if d == 3:
                numer_out[h, d - 1] = tokens_by_head(numer.astype(jnp.bfloat16))

                @pl.when(even)
                def _():
                    from_even(h)[0].start()

            else:

                @pl.when(even)
                def _():
                    kept_numer[h, d - 1] = numer

                @pl.when(jnp.logical_not(even))
                def _():
                    numer_out[h, d - 1] = tokens_by_head(numer.astype(jnp.bfloat16))

            @pl.when(jnp.logical_not(even))
            def _():
                from_odd(h)[d - 1].start()

        if h > 0:
            combine(h - 1)

    for c in local_kv:
        c.wait()
    for c in exchange_kv:
        c.wait_recv()
    n_rows = GROUP * tokens
    query_token = lax.broadcasted_iota(jnp.int32, (n_rows, tokens), 0) % tokens
    causal = lax.broadcasted_iota(jnp.int32, (n_rows, tokens), 1) <= query_token
    ones = jnp.ones((16, tokens), jnp.bfloat16)
    for h in range(heads):
        cols = slice(h * HEAD_SIZE, (h + 1) * HEAD_SIZE)
        fresh = jnp.where(causal, weigh(rows_by_head(qbufs[h][0]), k_own[:, cols]), 0.0)
        fresh = fresh.astype(jnp.bfloat16)
        own_numer[h] += jnp.dot(fresh, v_own[:, cols], preferred_element_type=jnp.float32)
        own_total[h] += lax.dot_general(
            ones, fresh, (((1,), (1,)), ((), ())), preferred_element_type=jnp.float32
        )[:8]

    combine(heads - 1)

    finished = []
    for h in range(heads):
        for c in totals_back[h]:
            c.wait_recv()
        send_numer(h, 1, numer_in.at[h, 0], 0, -1, 0).wait_recv()
        send_numer(h, 1, numer_in.at[h, 1], 1, -2, 0).wait_recv()
        total = own_total[h, 0:1, :]
        numer = own_numer[h]
        for d in range(1, SPAN):
            total = total + total_in[h, d - 1, d : d + 1, :]
        for d in range(2):
            numer = numer + rows_by_head(numer_in[h, d].astype(jnp.float32))
        per_row = jnp.broadcast_to(total, (128, n_rows)).T
        per_row = jnp.concatenate([per_row] * (HEAD_SIZE // 128), axis=1)
        done[h] = tokens_by_head((numer / per_row).astype(jnp.bfloat16))
        mine = pltpu.make_async_copy(
            done.at[h, my_rows, :], out.at[:, q_cols(t, h)], local_sem.at[heads + 2 + h]
        )
        mine.start()
        finished.append([mine])
        for i in range(1, n_tensor):
            their_rows = pl.ds(pl.multiple_of(tensor_at(i) * rows, rows), rows)
            c = remote(
                done.at[h, their_rows, :],
                out.at[:, q_cols(t, h)],
                ox_send.at[h, i],
                ox_recv.at[h, i],
                (p, tensor_at(i)),
            )
            c.start()
            finished[h].append(c)

    for h in range(heads):
        for c in exchange[h] + totals_back[h]:
            c.wait_send()

        @pl.when(even)
        def _():
            pass_query(h, 0, 1, 1, 0).wait_send()
            pass_query(h, 0, 2, 2, 1).wait_send()
            pass_query(h, 1, 2, 1, 2).wait_send()
            pass_query(h, 2, 3, 1, 3).wait_send()
            for c in from_even(h):
                c.wait_send()

        @pl.when(jnp.logical_not(even))
        def _():
            pass_query(h, 0, 1, 1, 0).wait_send()
            pass_query(h, 0, 3, 3, 1).wait_send()
            for c in from_odd(h):
                c.wait_send()

        for c in finished[h]:
            c.wait()
    for c in exchange_kv:
        c.wait_send()


def on_device(
    n_pool, n_tensor, queries, incoming_keys, incoming_values, k_pages, v_pages, page_table, lengths
):
    slots, page, cols = k_pages.shape
    heads = cols // HEAD_SIZE
    rows = queries.shape[0]
    tokens = rows * n_tensor
    holder = lax.axis_index("pool")
    global_slot = holder * slots + jnp.arange(slots, dtype=jnp.int32)
    matches = page_table[:, :, None] == global_slot[None, None, :]
    page_index = jnp.arange(page_table.shape[1], dtype=jnp.int32)[None, :, None]
    seen_all = jnp.sum(jnp.where(matches, lengths[:, None, None] - page_index * page, 0), axis=1)

    anywhere = pl.BlockSpec(memory_space=pltpu.HBM)
    dma = pltpu.SemaphoreType.DMA
    n_rows = GROUP * tokens
    bf16, f32 = jnp.bfloat16, jnp.float32
    scratch = [pltpu.VMEM((SPAN, tokens, WIDE), bf16) for _ in range(heads)] + [
        pltpu.VMEM((16, slots * page), bf16),
        pltpu.VMEM((SPAN, 16, slots * page), bf16),
        pltpu.VMEM((tokens, cols), bf16),
        pltpu.VMEM((tokens, cols), bf16),
        pltpu.VMEM((heads, slots, page, HEAD_SIZE), bf16),
        pltpu.VMEM((heads, slots, page, HEAD_SIZE), bf16),
        pltpu.VMEM((n_rows, slots * page), bf16),
        pltpu.VMEM((heads, n_rows, HEAD_SIZE), f32),
        pltpu.VMEM((heads, 8, n_rows), f32),
        pltpu.VMEM((heads, SPAN - 1, tokens, WIDE), bf16),
        pltpu.VMEM((heads, 8, n_rows), f32),
        pltpu.VMEM((heads, 2, tokens, WIDE), bf16),
        pltpu.VMEM((heads, SPAN - 1, 8, n_rows), f32),
        pltpu.VMEM((heads, 2, n_rows, HEAD_SIZE), f32),
        pltpu.VMEM((heads, 2, tokens, WIDE), bf16),
        pltpu.VMEM((heads, tokens, WIDE), bf16),
        dma((heads, 2)),
        dma((2 * heads + 2,)),
        dma((heads, n_tensor)),
        dma((heads, n_tensor)),
        dma((2, n_tensor)),
        dma((2, n_tensor)),
        dma((heads, SPAN)),
        dma((heads, SPAN)),
        dma((heads, SPAN)),
        dma((heads, SPAN)),
        dma((heads, SPAN)),
        dma((heads, SPAN)),
        dma((heads, n_tensor)),
        dma((heads, n_tensor)),
    ]
    return pl.pallas_call(
        functools.partial(kernel, n_pool, n_tensor, heads),
        out_shape=jax.ShapeDtypeStruct(queries.shape, queries.dtype),
        in_specs=[pl.BlockSpec(memory_space=pltpu.SMEM)] + [anywhere] * 5,
        out_specs=pl.BlockSpec(memory_space=pl.ANY),
        scratch_shapes=scratch,
        cost_estimate=pl.CostEstimate(
            flops=12 * heads * n_rows * slots * page * HEAD_SIZE,
            bytes_accessed=4 * slots * page * cols,
            transcendentals=2 * heads * n_rows * slots * page,
        ),
        compiler_params=pltpu.CompilerParams(
            collective_id=0, has_side_effects=True, vmem_limit_bytes=62 * 1024 * 1024
        ),
    )(
        seen_all,
        queries,
        incoming_keys,
        incoming_values,
        k_pages,
        v_pages,
    )


def solution(mesh):
    placed = (
        P(("pool", "tensor"), None),
        P(("pool", "tensor"), None),
        P(("pool", "tensor"), None),
        P("pool", None, "tensor"),
        P("pool", None, "tensor"),
        P(),
        P(),
    )
    return jax.shard_map(
        functools.partial(on_device, mesh.shape["pool"], mesh.shape["tensor"]),
        mesh=mesh,
        in_specs=placed,
        out_specs=P(("pool", "tensor"), None),
        check_vma=False,
    )
```

```python
import functools
import math

import jax
import jax.numpy as jnp
from jax import lax
from jax.experimental import pallas as pl
from jax.experimental.pallas import tpu as pltpu
from jax.sharding import PartitionSpec as P

QUERY_HEADS = 16
KEY_VALUE_HEADS = 8
HEAD_SIZE = 256
SPAN = 4
SOFTCAP = 50.0

GROUP = QUERY_HEADS // KEY_VALUE_HEADS
WIDE = GROUP * HEAD_SIZE
INNER = HEAD_SIZE ** (-0.5) / SOFTCAP
OUTER = SOFTCAP * math.log2(math.e)
MESH = pl.DeviceIdType.MESH


def rows_by_head(block):
    return jnp.concatenate(
        [block[:, g * HEAD_SIZE : (g + 1) * HEAD_SIZE] for g in range(GROUP)], axis=0
    )


def tokens_by_head(block):
    n = block.shape[0] // GROUP
    return jnp.concatenate([block[g * n : (g + 1) * n] for g in range(GROUP)], axis=1)


def weigh(query, key):
    dots = lax.dot_general(query, key, (((1,), (1,)), ((), ())), preferred_element_type=jnp.float32)
    return jnp.exp2(OUTER * jnp.tanh(dots * INNER))


def kernel(
    n_pool,
    n_tensor,
    heads,
    seen_all,
    q_in,
    k_in,
    v_in,
    k_pages,
    v_pages,
    out,
    *scratch,
):
    qbufs = scratch[:heads]
    (
        mask_rows,
        mask_each,
        k_own,
        v_own,
        k_mem,
        v_mem,
        weights,
        own_numer,
        own_total,
        numer_out,
        total_out,
        numer_in,
        total_in,
        kept_numer,
        relay_in,
        done,
        page_sem,
        local_sem,
        qx_send,
        qx_recv,
        kx_send,
        kx_recv,
        qf_send,
        qf_recv,
        nr_send,
        nr_recv,
        tr_send,
        tr_recv,
        ox_send,
        ox_recv,
    ) = scratch[heads:]
    p = lax.axis_index("pool")
    t = lax.axis_index("tensor")
    rows = q_in.shape[0]
    tokens = rows * n_tensor
    slots = k_pages.shape[0]
    page = k_pages.shape[1]
    span_cols = heads * HEAD_SIZE

    def pool_at(d):
        return (lax.rem(p + d + n_pool, n_pool), t)

    def tensor_at(i):
        return lax.rem(t + i, n_tensor)

    page_copies = []
    for h in range(heads):
        cols = slice(h * HEAD_SIZE, (h + 1) * HEAD_SIZE)
        page_copies.append(
            [
                pltpu.make_async_copy(k_pages.at[:, :, cols], k_mem.at[h], page_sem.at[h, 0]),
                pltpu.make_async_copy(v_pages.at[:, :, cols], v_mem.at[h], page_sem.at[h, 1]),
            ]
        )

    my_rows = pl.ds(pl.multiple_of(t * rows, rows), rows)

    def q_cols(owner, h):
        return pl.ds(pl.multiple_of((owner * heads + h) * WIDE, WIDE), WIDE)

    local = []
    for h in range(heads):
        local.append(
            pltpu.make_async_copy(
                q_in.at[:, q_cols(t, h)], qbufs[h].at[0, my_rows, :], local_sem.at[h]
            )
        )
    own_cols = pl.ds(pl.multiple_of(t * span_cols, span_cols), span_cols)
    local_kv = [
        pltpu.make_async_copy(k_in.at[:, own_cols], k_own.at[my_rows, :], local_sem.at[heads]),
        pltpu.make_async_copy(v_in.at[:, own_cols], v_own.at[my_rows, :], local_sem.at[heads + 1]),
    ]
    for c in local:
        c.start()
    for c in page_copies[0]:
        c.start()

    barrier = pltpu.get_barrier_semaphore()
    for i in range(1, n_tensor):
        pl.semaphore_signal(barrier, inc=1, device_id=(p, tensor_at(i)), device_id_type=MESH)
    for d in range(1, SPAN):
        pl.semaphore_signal(barrier, inc=1, device_id=pool_at(d), device_id_type=MESH)
        pl.semaphore_signal(barrier, inc=1, device_id=pool_at(-d), device_id_type=MESH)
    pl.semaphore_wait(barrier, n_tensor - 1 + 2 * (SPAN - 1))

    def remote(src, dst, send, recv, device):
        return pltpu.make_async_remote_copy(
            src_ref=src,
            dst_ref=dst,
            send_sem=send,
            recv_sem=recv,
            device_id=device,
            device_id_type=MESH,
        )

    exchange = []
    for h in range(heads):
        exchange.append(
            [
                remote(
                    q_in.at[:, q_cols(tensor_at(i), h)],
                    qbufs[h].at[0, my_rows, :],
                    qx_send.at[h, i],
                    qx_recv.at[h, i],
                    (p, tensor_at(i)),
                )
                for i in range(1, n_tensor)
            ]
        )
        for c in exchange[h]:
            c.start()
    exchange_kv = []
    for i in range(1, n_tensor):
        their_cols = pl.ds(pl.multiple_of(tensor_at(i) * span_cols, span_cols), span_cols)
        for j, (src, dst) in enumerate(((k_in, k_own), (v_in, v_own))):
            exchange_kv.append(
                remote(
                    src.at[:, their_cols],
                    dst.at[my_rows, :],
                    kx_send.at[j, i],
                    kx_recv.at[j, i],
                    (p, tensor_at(i)),
                )
            )
    for c in local_kv:
        c.start()
    for c in exchange_kv:
        c.start()
    for pair in page_copies[1:]:
        for c in pair:
            c.start()

    even = lax.rem(p, 2) == 0

    def pass_query(h, have, give, hop, sem):
        return remote(
            qbufs[h].at[have],
            qbufs[h].at[give],
            qf_send.at[h, sem],
            qf_recv.at[h, give],
            pool_at(hop),
        )

    for h in range(heads):
        local[h].wait()
        for c in exchange[h]:
            c.wait_recv()

        @pl.when(even)
        def _():
            pass_query(h, 0, 2, 2, 1).start()
            pass_query(h, 0, 1, 1, 0).start()

        @pl.when(jnp.logical_not(even))
        def _():
            pass_query(h, 0, 1, 1, 0).start()
            pass_query(h, 0, 3, 3, 1).start()

    def send_numer(h, d, dst, recv, hop, sem):
        return remote(
            numer_out.at[h, d - 1], dst, nr_send.at[h, sem], nr_recv.at[h, recv], pool_at(hop)
        )

    def from_even(h):
        return [
            send_numer(h, 3, numer_in.at[h, 1], 1, -3, 0),
            send_numer(h, 1, numer_in.at[h, 0], 0, -1, 1),
            send_numer(h, 2, numer_in.at[h, 1], 1, -2, 2),
        ]

    def from_odd(h):
        return [
            send_numer(h, 1, numer_in.at[h, 0], 0, -1, 0),
            send_numer(h, 2, relay_in.at[h, 0], 2, -1, 1),
            send_numer(h, 3, relay_in.at[h, 1], 3, -1, 2),
        ]

    def combine(h):
        @pl.when(even)
        def _():
            for d in (1, 2):
                from_odd(h)[d].wait_recv()
                both = kept_numer[h, d - 1] + rows_by_head(relay_in[h, d - 1].astype(jnp.float32))
                numer_out[h, d - 1] = tokens_by_head(both.astype(jnp.bfloat16))
                from_even(h)[d].start()

    seen = [[seen_all[lax.rem(p - d + n_pool, n_pool), s] for s in range(slots)] for d in range(SPAN)]
    dist = [
        sum(jnp.where(seen[d][s] > 0, d, 0).astype(jnp.int32) for d in range(1, SPAN))
        for s in range(slots)
    ]
    tile = (16, page)
    column = lax.broadcasted_iota(jnp.int32, tile, 1)
    row = lax.broadcasted_iota(jnp.int32, tile, 0)
    for s in range(slots):
        cols = slice(s * page, (s + 1) * page)
        by_row = jnp.zeros(tile, jnp.int32)
        for d in range(SPAN):
            mask_each[d, :, cols] = jnp.where(column < seen[d][s], 1.0, 0.0).astype(jnp.bfloat16)
            by_row = jnp.where(row == d, seen[d][s], by_row)
        mask_rows[:, cols] = jnp.where(column < by_row, 1.0, 0.0).astype(jnp.bfloat16)

    totals_back = []
    for h in range(heads):
        for c in page_copies[h]:
            c.wait()
        pass_query(h, 0, 1, 1, 0).wait_recv()

        @pl.when(even)
        def _():
            pass_query(h, 1, 2, 1, 2).start()

        pass_query(h, 0, 2, 2, 0).wait_recv()

        @pl.when(even)
        def _():
            pass_query(h, 2, 3, 1, 3).start()

        pass_query(h, 0, 3, 3, 0).wait_recv()

        qbuf = qbufs[h]

        for s in range(slots):
            query = rows_by_head(qbuf[dist[s]])
            cols = slice(s * page, (s + 1) * page)
            weights[:, cols] = weigh(query, k_mem[h, s]).astype(jnp.bfloat16)

        values = v_mem[h].reshape(slots * page, HEAD_SIZE)
        totals = lax.dot_general(
            mask_rows[...],
            weights[...],
            (((1,), (1,)), ((), ())),
            preferred_element_type=jnp.float32,
        )[:8]
        own_total[h] = totals
        total_out[h] = totals
        totals_back.append([])
        for d in range(1, SPAN):
            c = remote(
                total_out.at[h],
                total_in.at[h, d - 1],
                tr_send.at[h, d],
                tr_recv.at[h, d],
                pool_at(-d),
            )
            c.start()
            totals_back[h].append(c)
        for d in (3, 2, 1, 0):
            if d % 2 == 1:
                tiles = weights[...].reshape(-1, 16, slots * page)
                kept = [
                    (tiles * mask_each[e][None]).reshape(weights.shape) for e in (d, d - 1)
                ]
                two = jnp.dot(
                    jnp.concatenate(kept, axis=0), values, preferred_element_type=jnp.float32
                )
            half = weights.shape[0]
            numer = two[:half] if d % 2 == 1 else two[half:]
            if d == 0:
                own_numer[h] = numer
                continue
            if d == 3:
                numer_out[h, d - 1] = tokens_by_head(numer.astype(jnp.bfloat16))

                @pl.when(even)
                def _():
                    from_even(h)[0].start()

            else:

                @pl.when(even)
                def _():
                    kept_numer[h, d - 1] = numer

                @pl.when(jnp.logical_not(even))
                def _():
                    numer_out[h, d - 1] = tokens_by_head(numer.astype(jnp.bfloat16))

            @pl.when(jnp.logical_not(even))
            def _():
                from_odd(h)[d - 1].start()

        if h > 0:
            combine(h - 1)

    for c in local_kv:
        c.wait()
    for c in exchange_kv:
        c.wait_recv()
    n_rows = GROUP * tokens
    query_token = lax.broadcasted_iota(jnp.int32, (n_rows, tokens), 0) % tokens
    causal = lax.broadcasted_iota(jnp.int32, (n_rows, tokens), 1) <= query_token
    ones = jnp.ones((16, tokens), jnp.bfloat16)
    for h in range(heads):
        cols = slice(h * HEAD_SIZE, (h + 1) * HEAD_SIZE)
        fresh = jnp.where(causal, weigh(rows_by_head(qbufs[h][0]), k_own[:, cols]), 0.0)
        fresh = fresh.astype(jnp.bfloat16)
        own_numer[h] += jnp.dot(fresh, v_own[:, cols], preferred_element_type=jnp.float32)
        own_total[h] += lax.dot_general(
            ones, fresh, (((1,), (1,)), ((), ())), preferred_element_type=jnp.float32
        )[:8]

    combine(heads - 1)

    finished = []
    for h in range(heads):
        for c in totals_back[h]:
            c.wait_recv()
        send_numer(h, 1, numer_in.at[h, 0], 0, -1, 0).wait_recv()
        send_numer(h, 1, numer_in.at[h, 1], 1, -2, 0).wait_recv()
        total = own_total[h, 0:1, :]
        numer = own_numer[h]
        for d in range(1, SPAN):
            total = total + total_in[h, d - 1, d : d + 1, :]
        for d in range(2):
            numer = numer + rows_by_head(numer_in[h, d].astype(jnp.float32))
        per_row = jnp.broadcast_to(total, (128, n_rows)).T
        per_row = jnp.concatenate([per_row] * (HEAD_SIZE // 128), axis=1)
        done[h] = tokens_by_head((numer / per_row).astype(jnp.bfloat16))
        mine = pltpu.make_async_copy(
            done.at[h, my_rows, :], out.at[:, q_cols(t, h)], local_sem.at[heads + 2 + h]
        )
        mine.start()
        finished.append([mine])
        for i in range(1, n_tensor):
            their_rows = pl.ds(pl.multiple_of(tensor_at(i) * rows, rows), rows)
            c = remote(
                done.at[h, their_rows, :],
                out.at[:, q_cols(t, h)],
                ox_send.at[h, i],
                ox_recv.at[h, i],
                (p, tensor_at(i)),
            )
            c.start()
            finished[h].append(c)

    for h in range(heads):
        for c in exchange[h] + totals_back[h]:
            c.wait_send()

        @pl.when(even)
        def _():
            pass_query(h, 0, 1, 1, 0).wait_send()
            pass_query(h, 0, 2, 2, 1).wait_send()
            pass_query(h, 1, 2, 1, 2).wait_send()
            pass_query(h, 2, 3, 1, 3).wait_send()
            for c in from_even(h):
                c.wait_send()

        @pl.when(jnp.logical_not(even))
        def _():
            pass_query(h, 0, 1, 1, 0).wait_send()
            pass_query(h, 0, 3, 3, 1).wait_send()
            for c in from_odd(h):
                c.wait_send()

        for c in finished[h]:
            c.wait()
    for c in exchange_kv:
        c.wait_send()


def on_device(
    n_pool, n_tensor, queries, incoming_keys, incoming_values, k_pages, v_pages, page_table, lengths
):
    slots, page, cols = k_pages.shape
    heads = cols // HEAD_SIZE
    rows = queries.shape[0]
    tokens = rows * n_tensor
    holder = lax.axis_index("pool")
    global_slot = holder * slots + jnp.arange(slots, dtype=jnp.int32)
    matches = page_table[:, :, None] == global_slot[None, None, :]
    page_index = jnp.arange(page_table.shape[1], dtype=jnp.int32)[None, :, None]
    seen_all = jnp.sum(jnp.where(matches, lengths[:, None, None] - page_index * page, 0), axis=1)

    anywhere = pl.BlockSpec(memory_space=pltpu.HBM)
    dma = pltpu.SemaphoreType.DMA
    n_rows = GROUP * tokens
    bf16, f32 = jnp.bfloat16, jnp.float32
    scratch = [pltpu.VMEM((SPAN, tokens, WIDE), bf16) for _ in range(heads)] + [
        pltpu.VMEM((16, slots * page), bf16),
        pltpu.VMEM((SPAN, 16, slots * page), bf16),
        pltpu.VMEM((tokens, cols), bf16),
        pltpu.VMEM((tokens, cols), bf16),
        pltpu.VMEM((heads, slots, page, HEAD_SIZE), bf16),
        pltpu.VMEM((heads, slots, page, HEAD_SIZE), bf16),
        pltpu.VMEM((n_rows, slots * page), bf16),
        pltpu.VMEM((heads, n_rows, HEAD_SIZE), f32),
        pltpu.VMEM((heads, 8, n_rows), f32),
        pltpu.VMEM((heads, SPAN - 1, tokens, WIDE), bf16),
        pltpu.VMEM((heads, 8, n_rows), f32),
        pltpu.VMEM((heads, 2, tokens, WIDE), bf16),
        pltpu.VMEM((heads, SPAN - 1, 8, n_rows), f32),
        pltpu.VMEM((heads, 2, n_rows, HEAD_SIZE), f32),
        pltpu.VMEM((heads, 2, tokens, WIDE), bf16),
        pltpu.VMEM((heads, tokens, WIDE), bf16),
        dma((heads, 2)),
        dma((2 * heads + 2,)),
        dma((heads, n_tensor)),
        dma((heads, n_tensor)),
        dma((2, n_tensor)),
        dma((2, n_tensor)),
        dma((heads, SPAN)),
        dma((heads, SPAN)),
        dma((heads, SPAN)),
        dma((heads, SPAN)),
        dma((heads, SPAN)),
        dma((heads, SPAN)),
        dma((heads, n_tensor)),
        dma((heads, n_tensor)),
    ]
    return pl.pallas_call(
        functools.partial(kernel, n_pool, n_tensor, heads),
        out_shape=jax.ShapeDtypeStruct(queries.shape, queries.dtype),
        in_specs=[pl.BlockSpec(memory_space=pltpu.SMEM)] + [anywhere] * 5,
        out_specs=pl.BlockSpec(memory_space=pl.ANY),
        scratch_shapes=scratch,
        cost_estimate=pl.CostEstimate(
            flops=12 * heads * n_rows * slots * page * HEAD_SIZE,
            bytes_accessed=4 * slots * page * cols,
            transcendentals=2 * heads * n_rows * slots * page,
        ),
        compiler_params=pltpu.CompilerParams(
            collective_id=0, has_side_effects=True, vmem_limit_bytes=62 * 1024 * 1024
        ),
    )(
        seen_all,
        queries,
        incoming_keys,
        incoming_values,
        k_pages,
        v_pages,
    )


def solution(mesh):
    placed = (
        P(("pool", "tensor"), None),
        P(("pool", "tensor"), None),
        P(("pool", "tensor"), None),
        P("pool", None, "tensor"),
        P("pool", None, "tensor"),
        P(),
        P(),
    )
    return jax.shard_map(
        functools.partial(on_device, mesh.shape["pool"], mesh.shape["tensor"]),
        mesh=mesh,
        in_specs=placed,
        out_specs=P(("pool", "tensor"), None),
        check_vma=False,
    )
```
